32 devices in a mesh: slab: 2 (over y), dom: 4 (over z), coil: 4 (over x, core).
Axes of the slice: x: 2, y: 2, z: 4, core: 2. Of those that a mesh axis runs over, the one named last changes fastest.
Arguments:
- basis_image: bfloat16 [2, 5, 16, 128, 128], P(None, None, 'slab', 'dom'), parts along dimension 2, may hold values from -6 to 6
- coil_maps: bfloat16 [2, 48, 16, 128, 128], P(None, 'coil', 'slab', 'dom'), parts along dimension 2, may hold values from -1.5 to 1.5
- point_spread: float32 [32, 2, 256, 256], P(None, None, 'dom'), may hold values from -6 to 6
- basis_products: float32 [32, 2, 5, 5], replicated, may hold values from -0.625 to 0.625
- sampled: int32 [32, 8], replicated, may hold values 0 or 1
- adjoint_data: float32 [2, 5, 16, 128, 128], P(None, None, ('slab', 'coil'), 'dom'), parts along dimension 2, may hold values from -2 to 2
Outputs:
- gradient: float32 [2, 5, 16, 128, 128], P(None, None, ('slab', 'coil'), 'dom'), parts along dimension 2
The draws below stay inside these ranges and needn't reach their ends.
There are 2 independent parts, one for each index of `slab`. The reference program is written for one: setup_inputs(seed, part) draws one part's arguments, and reference() takes and returns one part's arrays. A program takes and returns all parts, laid end to end along the dimension named above; an argument that names none is the same for every part. Nothing has to cross between parts.
All inputs are finite; a program needn't handle non-finite values.
Results may differ from the reference program's by a relative error of at most 0.01.
Values may be sent and summed in bfloat16 or wider, within the bound.
No kernel may reach another device: no remote copies, remote signals or barrier semaphores. Data moves between devices by JAX's collectives and lax.ppermute only.
A program may use at most 128 MiB of HBM per device.

```python
import math
import jax
import jax.numpy as jnp
from jax import lax

K = 5
NZ = 8
NX = 128
NY = 128
C = 48
G = 32


def touch_ends(drawn, key, low, largest):
    place = [jax.random.randint(jax.random.fold_in(key, axis), (), 0, length) for axis, length in enumerate(drawn.shape)]
    longest = drawn.shape.index(max(drawn.shape))
    beside = place[:longest] + [(place[longest] + 1) % drawn.shape[longest]] + place[longest + 1:]
    return drawn.at[tuple(place)].set(low).at[tuple(beside)].set(largest)


def block_levels(rng, extent, split, smallest, high):
    def one(dim, blocks):
        draws = jax.random.uniform(jax.random.fold_in(jax.random.fold_in(rng, 6), dim), (blocks,), jnp.float32, smallest / len(split), high / len(split))
        return jnp.repeat(jnp.exp(draws), extent[dim] // blocks).reshape((-1,) + (1,) * (len(extent) - dim - 1))

    factor_of = one(*split[0])
    for cut in split[1:]:
        factor_of = factor_of * one(*cut)
    return factor_of


def noise(key, extent, spread, bound, cuts=(), kind=jnp.bfloat16):
    drawn = jax.random.normal(key, extent, jnp.float32) * spread
    if len(cuts) > 0:
        drawn = block_levels(key, extent, cuts, -0.22, 0.18) * drawn
    return jnp.clip(drawn, min=-bound, max=bound).astype(kind)


def setup_inputs(seed: int = 0, part: int = 0) -> dict:
    streams_of = jax.random.split(jax.random.key(seed), 7)
    own_keys = jax.random.split(jax.random.fold_in(streams_of[6], part), 7)
    basis_image = noise(own_keys[0], (2, K, NZ, NX, NY), 1.0, 6.0, ((3, 4),))
    coil_maps = noise(own_keys[1], (2, C, NZ, NX, NY), 0.25, 1.5, ((1, 4), (3, 4)))
    point_spread = noise(streams_of[2], (G, 2, 2 * NY, 2 * NX), 1.0, 6.0, ((2, 4),), jnp.float32)
    basis_products = noise(streams_of[3], (G, 2, K, K), (K * G // 2) ** -0.5, 0.625, (), jnp.float32)
    sampled = touch_ends((jax.random.randint(streams_of[4], (G, NZ), 0, 2) < 1).astype(jnp.int32), jax.random.fold_in(streams_of[4], 1), 0, 1)
    adjoint_data = noise(own_keys[5], (2, K, NZ, NX, NY), 0.3, 2.0, ((2, 4), (3, 4)), jnp.float32)
    return {"basis_image": basis_image, "coil_maps": coil_maps, "point_spread": point_spread, "basis_products": basis_products, "sampled": sampled, "adjoint_data": adjoint_data}


def dft_table(count_in, count_out, length, sign):
    first = jnp.arange(count_in, dtype=jnp.int32)
    second = jnp.arange(count_out, dtype=jnp.int32)
    phase = (first[:, None] * second[None, :] % length).astype(jnp.float32) * (2.0 * math.pi / length)
    scale = 1.0 / math.sqrt(length)
    cosine = jnp.cos(phase) * scale
    sine = jnp.sin(phase) * (sign * scale)
    table = jnp.stack([jnp.stack([cosine, -sine]), jnp.stack([sine, cosine])])
    return table.astype(jnp.bfloat16)

def build_kernel(sampled, basis_products, point_spread):
    weights = basis_products[:, :, :, :, None] * sampled.astype(jnp.float32)[:, None, None, None, :]
    high = lax.Precision.HIGHEST
    kernel_real = jnp.einsum('gkjq,gvu->kjqvu', weights[:, 0], point_spread[:, 0], precision=high) - jnp.einsum('gkjq,gvu->kjqvu', weights[:, 1], point_spread[:, 1], precision=high)
    kernel_imag = jnp.einsum('gkjq,gvu->kjqvu', weights[:, 0], point_spread[:, 1], precision=high) + jnp.einsum('gkjq,gvu->kjqvu', weights[:, 1], point_spread[:, 0], precision=high)
    return (kernel_real, kernel_imag)

def apply_kernel(kernel_real, kernel_imag, spectrum):
    real_acc = jnp.zeros(spectrum.shape[1:], jnp.float32)
    imag_acc = jnp.zeros(spectrum.shape[1:], jnp.float32)
    for column in range(spectrum.shape[2]):
        real_in = spectrum[0][:, column][:, None]
        imag_in = spectrum[1][:, column][:, None]
        real_acc = real_acc + kernel_real[:, column][None] * real_in - kernel_imag[:, column][None] * imag_in
        imag_acc = imag_acc + kernel_real[:, column][None] * imag_in + kernel_imag[:, column][None] * real_in
    return jnp.stack([real_acc, imag_acc])

def transform(table, data, form):
    return jnp.einsum(form, table.astype(jnp.float32), data.astype(jnp.float32))

def reference(basis_image, coil_maps, point_spread, basis_products, sampled, adjoint_data):
    forward_z = dft_table(NZ, NZ, NZ, -1)
    forward_y = dft_table(NY, 2 * NY, 2 * NY, -1)
    forward_x = dft_table(NX, 2 * NX, 2 * NX, -1)
    inverse_x = dft_table(2 * NX, NX, 2 * NX, 1)
    inverse_y = dft_table(2 * NY, NY, 2 * NY, 1)
    inverse_z = dft_table(NZ, NZ, NZ, 1)
    kernel_real, kernel_imag = build_kernel(sampled, basis_products, point_spread)
    image_f = basis_image.astype(jnp.float32)

    def one_coil(index, total):
        maps_now = lax.dynamic_slice_in_dim(coil_maps, index, 1, 1).astype(jnp.float32)
        coil_real = maps_now[0][:, None] * image_f[0][None] - maps_now[1][:, None] * image_f[1][None]
        coil_imag = maps_now[0][:, None] * image_f[1][None] + maps_now[1][:, None] * image_f[0][None]
        coil_image = jnp.stack([coil_real, coil_imag]).astype(jnp.bfloat16)
        partition = transform(forward_z, coil_image, 'oizq,ibkzry->obkqry').astype(jnp.bfloat16)
        rows = transform(forward_y, partition, 'oiyw,ibkqry->obkqrw').astype(jnp.bfloat16)
        spectrum = transform(forward_x, rows, 'oixu,ibkqxw->obkqwu')
        weighted = apply_kernel(kernel_real, kernel_imag, spectrum).astype(jnp.bfloat16)
        columns = transform(inverse_x, weighted, 'oiux,ibkqwu->obkqwx').astype(jnp.bfloat16)
        back_rows = transform(inverse_y, columns, 'oiwy,ibkqwr->obkqry').astype(jnp.bfloat16)
        coil_back = transform(inverse_z, back_rows, 'oiqz,ibkqry->obkzry')
        grad_real = lax.optimization_barrier(jnp.sum(maps_now[0][:, None] * coil_back[0] + maps_now[1][:, None] * coil_back[1], axis=0))
        grad_imag = lax.optimization_barrier(jnp.sum(maps_now[0][:, None] * coil_back[1] - maps_now[1][:, None] * coil_back[0], axis=0))
        return total + jnp.stack([grad_real, grad_imag])
    zeros = jnp.zeros((2, K, NZ, NX, NY), jnp.float32)
    total = lax.fori_loop(0, C, one_coil, zeros)
    return total - adjoint_data
```

```python
import functools
import math

import jax
import jax.numpy as jnp
import numpy as np
from jax import lax
from jax.experimental import pallas as pl
from jax.experimental.pallas import tpu as pltpu
from jax.sharding import PartitionSpec as P

K = 5
NZ = 8
BF = jnp.bfloat16
F32 = jnp.float32
HALF = math.sqrt(0.5)


def table(count_in, count_out, length, sign):
    phase = (np.arange(count_in)[:, None] * np.arange(count_out)[None, :] % length).astype(
        np.float32
    ) * np.float32(2.0 * math.pi / length)
    scale = 1.0 / math.sqrt(length)
    cosine = np.cos(phase) * np.float32(scale)
    sine = np.sin(phase) * np.float32(sign * scale)
    return np.stack([np.stack([cosine, -sine]), np.stack([sine, cosine])]).astype(BF)


def add(a, b):
    return (a[0] + b[0], a[1] + b[1])


def sub(a, b):
    return (a[0] - b[0], a[1] - b[1])


def add_turned(a, b, sign):
    return (a[0] - b[1], a[1] + b[0]) if sign > 0 else (a[0] + b[1], a[1] - b[0])


def four(v, sign):
    a, b = add(v[0], v[2]), sub(v[0], v[2])
    c, d = add(v[1], v[3]), sub(v[1], v[3])
    return [add(a, c), add_turned(b, d, sign), sub(a, c), add_turned(b, d, -sign)]


def eight(re, im, sign):
    v = list(zip(re, im))
    e, o = four(v[0::2], sign), four(v[1::2], sign)
    h = jnp.asarray(HALF, re[0].dtype)
    once = add_turned(o[1], o[1], sign)
    once = (once[0] * h, once[1] * h)
    thrice = add_turned((-o[3][0], -o[3][1]), o[3], sign)
    thrice = (thrice[0] * h, thrice[1] * h)
    out = [None] * 8
    for q, t in ((0, o[0]), (1, once), (3, thrice)):
        out[q], out[q + 4] = add(e[q], t), sub(e[q], t)
    out[2], out[6] = add_turned(e[2], o[2], sign), add_turned(e[2], o[2], -sign)
    return [x[0] for x in out], [x[1] for x in out]


def tree(terms):
    while len(terms) > 1:
        terms = [
            terms[i] + terms[i + 1] if i + 1 < len(terms) else terms[i]
            for i in range(0, len(terms), 2)
        ]
    return terms[0]


def coils_kernel(width, pieces, first, last, *refs):
    maps = refs[:pieces]
    image, weights_hbm, ty, tx, tix, tiy = refs[pieces : pieces + 6]
    rest = list(refs[pieces + 6 :])
    acc_in = None if first else rest.pop(0)
    out = rest.pop(0)
    rows, spec, mid, weights, sem = rest[:5]
    acc = rest[5] if last else out
    tiles = width // 16
    step = pl.program_id(0)
    fetch = pltpu.make_async_copy(weights_hbm, weights, sem)

    @pl.when(step == 0)
    def _():
        fetch.start()
        acc[...] = jnp.zeros_like(acc) if first else acc_in[...]

    def maps_of(part, z):
        return jnp.concatenate([m[part, 0, z] for m in maps], axis=0)

    def forward(j, _):
        for z in range(NZ):
            mr, mi = maps_of(0, z), maps_of(1, z)
            ir = jnp.concatenate([image[r, 0, j, z] for r in range(pieces)], axis=0)
            ii = jnp.concatenate([image[r, 1, j, z] for r in range(pieces)], axis=0)
            product = jnp.concatenate([mr * ir - mi * ii, mr * ii + mi * ir], axis=1)
            rows[z] = jnp.dot(product, ty[...], preferred_element_type=F32).astype(BF).T
        for t in range(tiles):
            a, b = pl.ds(t * 16, 16), pl.ds(width + t * 16, 16)
            re, im = eight(
                [rows[z, a].astype(F32) for z in range(NZ)],
                [rows[z, b].astype(F32) for z in range(NZ)],
                -1,
            )
            for q in range(NZ):
                mid[q, a] = jnp.concatenate([re[q], im[q]], axis=1).astype(BF)
        for q in range(NZ):
            spec[j, q] = jnp.dot(mid[q], tx[...], preferred_element_type=F32).astype(BF)
        return 0

    lax.fori_loop(0, K, forward, 0)

    @pl.when(step == 0)
    def _():
        fetch.wait()

    half = tx.shape[1] // 2

    def apply(i, _):
        q = i // tiles
        a = pl.ds(pl.multiple_of(i % tiles * 16, 16), 16)
        sr = [spec[j, q, a, :half] for j in range(K)]
        si = [spec[j, q, a, half:] for j in range(K)]
        for k in range(K):
            re, im = [], []
            for j in range(K):
                kr, ki = weights[q, k, j, 0, a], weights[q, k, j, 1, a]
                re.append(kr * sr[j] - ki * si[j])
                im.append(kr * si[j] + ki * sr[j])
            spec[k, q, a, :half] = tree(re)
            spec[k, q, a, half:] = tree(im)
        return 0

    lax.fori_loop(0, NZ * tiles, apply, 0)
    ny = tiy.shape[1] // 2
    nx = tix.shape[1] // 2

    def inverse(k, _):
        for q in range(NZ):
            mid[q] = jnp.dot(spec[k, q], tix[...], preferred_element_type=F32).astype(BF)
        for t in range(tiles):
            a, b = pl.ds(t * 16, 16), pl.ds(width + t * 16, 16)
            re, im = eight(
                [mid[q, a, :nx].astype(F32) for q in range(NZ)],
                [mid[q, a, nx:].astype(F32) for q in range(NZ)],
                1,
            )
            for z in range(NZ):
                rows[z, a] = re[z].astype(BF)
                rows[z, b] = im[z].astype(BF)
        for z in range(NZ):
            back = jnp.dot(rows[z].T, tiy[...], preferred_element_type=F32)
            br, bi = back[:, :ny], back[:, ny:]
            mr, mi = maps_of(0, z).astype(F32), maps_of(1, z).astype(F32)
            acc[z, 0, k] += mr * br + mi * bi
            acc[z, 1, k] += mr * bi - mi * br
        return 0

    lax.fori_loop(0, K, inverse, 0)
    if last:

        @pl.when(step == pl.num_programs(0) - 1)
        def _():
            out[...] = acc[...].astype(BF)


def coils(maps, image, weights, tables, acc, last):
    count = maps[0].shape[1]
    width = tables[0].shape[1] // 2
    nx, ny = tables[2].shape[1] // 2, tables[3].shape[1] // 2
    pieces = len(maps)
    whole = lambda a: pl.BlockSpec(
        a.shape, lambda c: (0,) * a.ndim, pipeline_mode=pl.Buffered(buffer_count=1)
    )
    shape = (NZ, 2, K, nx, ny)
    out = jax.ShapeDtypeStruct(shape, BF if last else F32)
    args = [*maps, image, weights, *tables]
    specs = [pl.BlockSpec((2, 1) + m.shape[2:], lambda c: (0, c, 0, 0, 0)) for m in maps]
    specs += [whole(image), pl.BlockSpec(memory_space=pl.ANY)] + [whole(t) for t in tables]
    if acc is not None:
        args.append(acc)
        specs.append(whole(acc))
    scratch = [
        pltpu.VMEM((NZ, 2 * width, nx), BF),
        pltpu.VMEM((K, NZ, width, tables[1].shape[1]), BF),
        pltpu.VMEM((NZ, width, 2 * nx), BF),
        pltpu.VMEM(weights.shape, BF),
        pltpu.SemaphoreType.DMA,
    ]
    if last:
        scratch.append(pltpu.VMEM(shape, F32))
    planes = count * K * NZ
    return pl.pallas_call(
        functools.partial(coils_kernel, width, pieces, acc is None, last),
        grid=(count,),
        in_specs=specs,
        out_specs=whole(out),
        out_shape=out,
        scratch_shapes=scratch,
        compiler_params=pltpu.CompilerParams(vmem_limit_bytes=60 * 2**20),
        cost_estimate=pl.CostEstimate(
            flops=planes * width * 4 * 2 * 200_000, bytes_accessed=30_000_000, transcendentals=0
        ),
    )(*args)


def kernel_weights(sampled, basis_products, point_spread, pad):
    scale = float(table(1, 1, NZ, 1)[0, 0, 0, 0].astype(np.float32)) ** 2
    picked = basis_products[:, :, :, :, None] * (
        sampled.astype(F32)[:, None, None, None, :] * scale
    )
    real, imag = picked[:, 0], picked[:, 1]
    pairs = jnp.stack([jnp.stack([real, -imag], 1), jnp.stack([imag, real], 1)], 1)
    spread = point_spread.astype(BF)
    if pad:
        spread = jnp.pad(spread, ((0, 0), (0, 0), (0, pad), (0, 0)))
    return jnp.einsum(
        "gpikjq,givu->qkjpvu", pairs.astype(BF), spread, preferred_element_type=F32
    ).astype(BF)


def swap(value, axis, bit):
    size = lax.axis_size(axis)
    return lax.ppermute(value, axis, [(i, i ^ bit) for i in range(size)])


def gather_rows(value, axis):
    one, two = swap(value, axis, 1), swap(value, axis, 2)
    return [value, one, two, swap(two, axis, 1)]


def body(basis_image, coil_maps, point_spread, basis_products, sampled, adjoint_data):
    dom, here = lax.axis_size("dom"), lax.axis_index("dom")
    coil, me = lax.axis_size("coil"), lax.axis_index("coil")
    rows, ny = basis_image.shape[3], basis_image.shape[4]
    nx = rows * dom
    own = point_spread.shape[2]
    width = max(64, own)
    butterfly = dom == 4 and coil == 4 and rows % 16 == 0

    forward, inverse = table(nx, 2 * nx, 2 * nx, -1), table(2 * nx, nx, 2 * nx, 1)
    tx = forward.transpose(1, 2, 0, 3)
    tix = inverse.transpose(1, 2, 0, 3)
    forward, inverse = table(ny, 2 * ny, 2 * ny, -1), table(2 * ny, ny, 2 * ny, 1)
    extra = ((0, 0), (0, 0), (0, 0), (0, width - own))
    ty = np.pad(forward.transpose(1, 2, 0, 3), extra)
    tiy = np.pad(inverse.transpose(1, 3, 0, 2), extra).transpose(0, 3, 2, 1)
    ty = lax.dynamic_slice_in_dim(jnp.asarray(ty), here * own, width, 3).reshape(2 * ny, 2 * width)
    tiy = lax.dynamic_slice_in_dim(jnp.asarray(tiy), here * own, width, 1).reshape(
        2 * width, 2 * ny
    )
    weights = kernel_weights(sampled, basis_products, point_spread, width - own)

    if butterfly:
        order = here ^ jnp.arange(dom)
        tx = jnp.take(jnp.asarray(tx.reshape(2, dom, rows, -1)), order, axis=1)
        tix = jnp.take(jnp.asarray(tix.reshape(2 * 2 * nx * 2, dom, rows)), order, axis=1)
        core = me % 2
        mine = lax.dynamic_slice_in_dim(basis_image, core * (NZ // 2), NZ // 2, 2)
        mine = jnp.stack(gather_rows(mine, "dom"))
        other = swap(mine, "coil", 1)
        image = jnp.concatenate(
            [jnp.where(core == 0, mine, other), jnp.where(core == 0, other, mine)], axis=3
        )
        chunks = CHUNKS
    else:
        image = lax.all_gather(basis_image, "dom", axis=3, tiled=True)[None]
        chunks = (coil_maps.shape[1],)
    tx, tix = jnp.asarray(tx).reshape(2 * nx, 4 * nx), jnp.asarray(tix).reshape(4 * nx, 2 * nx)
    tables = (ty, tx, tix, tiy)

    total, start = None, 0
    for count in chunks:
        part = lax.slice_in_dim(coil_maps, start, start + count, axis=1)
        start += count
        if butterfly:
            maps = gather_rows(part, "dom")
        else:
            maps = [lax.all_gather(part, "dom", axis=3, tiled=True)]
        total = coils(maps, image, weights, tables, total, start == coil_maps.shape[1])

    if not butterfly:
        total = lax.psum_scatter(total.transpose(1, 2, 0, 3, 4), "coil", scatter_dimension=2, tiled=True)
        total = lax.psum_scatter(total, "dom", scatter_dimension=3, tiled=True)
        return total.astype(F32) - adjoint_data

    def exchange(value, dim, bit, axis, index):
        send = lax.dynamic_index_in_dim(value, 1 - index, dim, keepdims=False)
        keep = lax.dynamic_index_in_dim(value, index, dim, keepdims=False)
        return keep.astype(F32) + swap(send.astype(BF), axis, bit).astype(F32)

    total = total.reshape(coil // 2, 2, NZ // coil, 2, K, dom // 2, 2, rows, ny)
    total = exchange(total, 1, 1, "coil", me % 2)
    total = exchange(total.astype(BF), 0, 2, "coil", me // 2)
    total = total.astype(BF)
    keep, send = total[:, :, :, :, 0], total[:, :, :, :, 1]
    total = (keep.astype(F32) + swap(send, "dom", 1).astype(F32)).astype(BF)
    keep, send = total[:, :, :, 0], total[:, :, :, 1]
    total = keep.astype(F32) + swap(send, "dom", 2).astype(F32)
    return total.transpose(1, 2, 0, 3, 4) - adjoint_data


CHUNKS = (3, 3, 3, 3)


def solution(mesh):
    placed = (
        P(None, None, "slab", "dom", None),
        P(None, "coil", "slab", "dom", None),
        P(None, None, "dom", None),
        P(),
        P(),
        P(None, None, ("slab", "coil"), "dom", None),
    )
    return jax.shard_map(
        body,
        mesh=mesh,
        in_specs=placed,
        out_specs=P(None, None, ("slab", "coil"), "dom", None),
        check_vma=False,
    )
```

```python
import functools
import math

import jax
import jax.numpy as jnp
import numpy as np
from jax import lax
from jax.experimental import pallas as pl
from jax.experimental.pallas import tpu as pltpu
from jax.sharding import PartitionSpec as P

K = 5
NZ = 8
BF = jnp.bfloat16
F32 = jnp.float32
HALF = math.sqrt(0.5)


def table(count_in, count_out, length, sign):
    phase = (np.arange(count_in)[:, None] * np.arange(count_out)[None, :] % length).astype(
        np.float32
    ) * np.float32(2.0 * math.pi / length)
    scale = 1.0 / math.sqrt(length)
    cosine = np.cos(phase) * np.float32(scale)
    sine = np.sin(phase) * np.float32(sign * scale)
    return np.stack([np.stack([cosine, -sine]), np.stack([sine, cosine])]).astype(BF)


def add(a, b):
    return (a[0] + b[0], a[1] + b[1])


def sub(a, b):
    return (a[0] - b[0], a[1] - b[1])


def add_turned(a, b, sign):
    return (a[0] - b[1], a[1] + b[0]) if sign > 0 else (a[0] + b[1], a[1] - b[0])


def four(v, sign):
    a, b = add(v[0], v[2]), sub(v[0], v[2])
    c, d = add(v[1], v[3]), sub(v[1], v[3])
    return [add(a, c), add_turned(b, d, sign), sub(a, c), add_turned(b, d, -sign)]


def eight(re, im, sign):
    v = list(zip(re, im))
    e, o = four(v[0::2], sign), four(v[1::2], sign)
    h = jnp.asarray(HALF, re[0].dtype)
    once = add_turned(o[1], o[1], sign)
    once = (once[0] * h, once[1] * h)
    thrice = add_turned((-o[3][0], -o[3][1]), o[3], sign)
    thrice = (thrice[0] * h, thrice[1] * h)
    out = [None] * 8
    for q, t in ((0, o[0]), (1, once), (3, thrice)):
        out[q], out[q + 4] = add(e[q], t), sub(e[q], t)
    out[2], out[6] = add_turned(e[2], o[2], sign), add_turned(e[2], o[2], -sign)
    return [x[0] for x in out], [x[1] for x in out]


def tree(terms):
    while len(terms) > 1:
        terms = [
            terms[i] + terms[i + 1] if i + 1 < len(terms) else terms[i]
            for i in range(0, len(terms), 2)
        ]
    return terms[0]


def coils_kernel(width, pieces, images, first, last, where, *refs):
    maps, refs = refs[:pieces], refs[pieces:]
    shared, refs = refs[:images], refs[images:]
    weights_hbm, ty, tx, tix, tiy = refs[:5]
    rest = list(refs[5:])
    acc_in = None if first else rest.pop(0)
    outs, rest = (rest[:2], rest[2:]) if last else (rest[:1], rest[1:])
    image, rows, spec, mid, product, weights, sems, image_sems = rest[:8]
    acc = rest[8] if last else outs[0]
    nx, ny = tix.shape[1] // 2, tiy.shape[1] // 2
    tiles = width // 16
    step = pl.program_id(0)
    me = where[1]
    fetch = [
        pltpu.make_async_copy(weights_hbm.at[q], weights.at[q], sems.at[q]) for q in range(NZ)
    ]
    resume = None if first else pltpu.make_async_copy(acc_in, acc, sems.at[NZ])
    groups = image.shape[0]
    arrive = []
    for b, ref in enumerate(shared):
        for x in range(ref.shape[0]):
            slot = ((x ^ (me // 2)) * 2 + (b ^ (me % 2))) if groups > 1 else 0
            arrive.append(
                pltpu.make_async_copy(ref.at[x], image.at[slot], image_sems.at[len(arrive)])
            )

    @pl.when(step == 0)
    def _():
        for copy in arrive:
            copy.start()
        for copy in fetch:
            copy.start()
        if first:
            acc[...] = jnp.zeros_like(acc)
        else:
            resume.start()
        for copy in arrive:
            copy.wait()

    def image_of(part, j, z):
        group, plane = z // (NZ // groups), z % (NZ // groups)
        return jnp.concatenate(
            [image[group, r, part, j, plane] for r in range(image.shape[1])], axis=0
        )

    def maps_of(part, z):
        return jnp.concatenate([m[part, 0, z] for m in maps], axis=0)

    def forward(j, _):
        for z in range(NZ):
            mr, mi = maps_of(0, z), maps_of(1, z)
            ir, ii = image_of(0, j, z), image_of(1, j, z)
            product[j, z * nx : (z + 1) * nx] = jnp.concatenate(
                [mr * ir - mi * ii, mr * ii + mi * ir], axis=1
            )
        turned = jnp.dot(product[j], ty[...], preferred_element_type=F32).astype(BF)
        for z in range(NZ):
            rows[j, z] = turned[z * nx : (z + 1) * nx].T
        for t in range(tiles):
            a, b = pl.ds(t * 16, 16), pl.ds(width + t * 16, 16)
            re, im = eight(
                [rows[j, z, a].astype(F32) for z in range(NZ)],
                [rows[j, z, b].astype(F32) for z in range(NZ)],
                -1,
            )
            for q in range(NZ):
                mid[j, pl.ds(q * width + t * 16, 16)] = jnp.concatenate(
                    [re[q], im[q]], axis=1
                ).astype(BF)
        spec[j] = jnp.dot(mid[j], tx[...], preferred_element_type=F32).astype(BF)
        return 0

    for j in range(K):
        forward(j, 0)

    half = tx.shape[1] // 2

    def apply(q, t):
        a = pl.ds(t * 16, 16)
        at = pl.ds(pl.multiple_of(q * width + t * 16, 16), 16)
        sr = [spec[j, at, :half] for j in range(K)]
        si = [spec[j, at, half:] for j in range(K)]
        for k in range(K):
            re, im = [], []
            for j in range(K):
                kr, ki = weights[q, k, j, 0, a], weights[q, k, j, 1, a]
                re.append(kr * sr[j] - ki * si[j])
                im.append(kr * si[j] + ki * sr[j])
            spec[k, at, :half] = tree(re)
            spec[k, at, half:] = tree(im)

    def apply_all(q, _):
        @pl.when(step == 0)
        def _():
            pltpu.make_async_copy(weights_hbm.at[q], weights.at[q], sems.at[q]).wait()

        for t in range(tiles):
            apply(q, t)
        return 0

    lax.fori_loop(0, NZ, apply_all, 0)
    if not first:

        @pl.when(step == 0)
        def _():
            resume.wait()


    def inverse(k, _):
        mid[k] = jnp.dot(spec[k], tix[...], preferred_element_type=F32).astype(BF)
        for t in range(tiles):
            a, b = pl.ds(t * 16, 16), pl.ds(width + t * 16, 16)
            re, im = eight(
                [mid[k, pl.ds(q * width + t * 16, 16), :nx].astype(F32) for q in range(NZ)],
                [mid[k, pl.ds(q * width + t * 16, 16), nx:].astype(F32) for q in range(NZ)],
                1,
            )
            for z in range(NZ):
                rows[k, z, a] = re[z].astype(BF)
                rows[k, z, b] = im[z].astype(BF)
        turned = jnp.concatenate([rows[k, z].T for z in range(NZ)], axis=0)
        backs = jnp.dot(turned, tiy[...], preferred_element_type=F32)
        for z in range(NZ):
            back = backs[z * nx : (z + 1) * nx]
            br, bi = back[:, :ny], back[:, ny:]
            mr, mi = maps_of(0, z).astype(F32), maps_of(1, z).astype(F32)
            acc[z, 0, k] += mr * br + mi * bi
            acc[z, 1, k] += mr * bi - mi * br
        return 0

    for k in range(K):
        inverse(k, 0)
    if last:

        @pl.when(step == pl.num_programs(0) - 1)
        def _():
            for x in range(2):
                for z in range(NZ // 4):
                    base = (x ^ (me // 2)) * (NZ // 2) + z
                    for c in range(2):
                        outs[c][x, z] = acc[base + (c ^ (me % 2)) * (NZ // 4)].astype(BF)


def coils(maps, images, weights, tables, acc, last, where):
    count = maps[0].shape[1]
    spec_width = tables[1].shape[2]
    width = tables[0].shape[2] // 2
    nx, ny = tables[2].shape[2] // 2, tables[3].shape[2] // 2
    anywhere = pl.BlockSpec(memory_space=pl.ANY)
    shape = (NZ, 2, K, nx, ny)
    half = (2, NZ // 4, 2, K, nx, ny)
    out = [jax.ShapeDtypeStruct(half, BF)] * 2 if last else jax.ShapeDtypeStruct(shape, F32)
    block = lambda dims: pl.BlockSpec(
        dims, lambda c, w: (0,) * len(dims), pipeline_mode=pl.Buffered(buffer_count=1)
    )
    args = [*maps, *images, weights, *tables]
    specs = [pl.BlockSpec((2, 1) + m.shape[2:], lambda c, w: (0, c, 0, 0, 0)) for m in maps]
    specs += [anywhere] * (len(images) + 1)
    specs += [
        pl.BlockSpec(
            (None,) + t.shape[1:],
            lambda c, w: (w[0], 0, 0),
            pipeline_mode=pl.Buffered(buffer_count=1),
        )
        for t in tables
    ]
    if acc is not None:
        args.append(acc)
        specs.append(anywhere)
    groups = sum(i.shape[0] for i in images)
    scratch = [
        pltpu.VMEM((groups,) + images[0].shape[1:], BF),
        pltpu.VMEM((K, NZ, 2 * width, nx), BF),
        pltpu.VMEM((K, NZ * width, spec_width), BF),
        pltpu.VMEM((K, NZ * width, 2 * nx), BF),
        pltpu.VMEM((K, NZ * nx, 2 * ny), BF),
        pltpu.VMEM(weights.shape, BF),
        pltpu.SemaphoreType.DMA((NZ + 1,)),
        pltpu.SemaphoreType.DMA((groups,)),
    ]
    if last:
        scratch.append(pltpu.VMEM(shape, F32))
    planes = count * K * NZ
    return pl.pallas_call(
        functools.partial(coils_kernel, width, len(maps), len(images), acc is None, last),
        grid_spec=pltpu.PrefetchScalarGridSpec(
            num_scalar_prefetch=1,
            grid=(count,),
            in_specs=specs,
            out_specs=[block(half)] * 2 if last else block(shape),
            scratch_shapes=scratch,
        ),
        out_shape=out,
        compiler_params=pltpu.CompilerParams(vmem_limit_bytes=60 * 2**20),
        cost_estimate=pl.CostEstimate(
            flops=planes * width * 4 * 2 * 200_000, bytes_accessed=30_000_000, transcendentals=0
        ),
    )(where, *args)


def kernel_weights(sampled, basis_products, point_spread, pad):
    scale = float(table(1, 1, NZ, 1)[0, 0, 0, 0].astype(np.float32)) ** 2
    picked = basis_products[:, :, :, :, None] * (
        sampled.astype(F32)[:, None, None, None, :] * scale
    )
    real, imag = picked[:, 0], picked[:, 1]
    pairs = jnp.stack([jnp.stack([real, -imag], 1), jnp.stack([imag, real], 1)], 1)
    spread = point_spread.astype(BF)
    if pad:
        spread = jnp.pad(spread, ((0, 0), (0, 0), (0, pad), (0, 0)))
    return jnp.einsum(
        "gpikjq,givu->qkjpvu", pairs.astype(BF), spread, preferred_element_type=F32
    ).astype(BF)


def swap(value, axis, bit):
    size = lax.axis_size(axis)
    return lax.ppermute(value, axis, [(i, i ^ bit) for i in range(size)])


def body(basis_image, coil_maps, point_spread, basis_products, sampled, adjoint_data):
    dom, here = lax.axis_size("dom"), lax.axis_index("dom")
    coil, me = lax.axis_size("coil"), lax.axis_index("coil")
    rows, ny = basis_image.shape[3], basis_image.shape[4]
    nx = rows * dom
    own = point_spread.shape[2]
    width = max(64, own)
    butterfly = dom == 4 and rows % 16 == 0

    forward, inverse = table(ny, 2 * ny, 2 * ny, -1), table(2 * ny, ny, 2 * ny, 1)
    extra = ((0, 0), (0, 0), (0, 0), (0, width - own))
    forward = np.pad(forward.transpose(1, 2, 0, 3), extra)
    inverse = np.pad(inverse.transpose(1, 0, 3, 2), extra).transpose(0, 3, 1, 2)
    ty = np.stack([forward[..., d * own : d * own + width] for d in range(dom)])
    tiy = np.stack([inverse[:, d * own : d * own + width] for d in range(dom)])
    forward, inverse = table(nx, 2 * nx, 2 * nx, -1), table(2 * nx, nx, 2 * nx, 1)
    tx = forward.transpose(1, 2, 0, 3).reshape(2, dom, rows, 4 * nx)
    tix = inverse.transpose(1, 2, 0, 3).reshape(4 * nx, 2, dom, rows)
    orders = [[d ^ r for r in range(dom)] if butterfly else range(dom) for d in range(dom)]
    if not butterfly:
        orders = orders[:1]
    tx = np.stack([tx[:, list(o)] for o in orders])
    tix = np.stack([tix[:, :, list(o)] for o in orders])
    if not butterfly:
        ty = lax.dynamic_slice_in_dim(jnp.asarray(ty), here, 1, 0)
        tiy = lax.dynamic_slice_in_dim(jnp.asarray(tiy), here, 1, 0)
    tables = [
        jnp.asarray(ty).reshape(-1, 2 * ny, 2 * width),
        jnp.asarray(tx).reshape(-1, 2 * nx, 4 * nx),
        jnp.asarray(tix).reshape(-1, 4 * nx, 2 * nx),
        jnp.asarray(tiy).reshape(-1, 2 * width, 2 * ny),
    ]
    where = jnp.stack([here if butterfly else 0 * here, me]).astype(jnp.int32)
    weights = kernel_weights(sampled, basis_products, point_spread, width - own)
    count = coil_maps.shape[1]

    if butterfly:
        sizes = CHUNKS if sum(CHUNKS) == count else (count,)
        starts = [sum(sizes[:m]) for m in range(len(sizes))]
        parts = [
            lax.slice_in_dim(coil_maps, a, a + n, axis=1) for a, n in zip(starts, sizes)
        ] + [None, None]

        def begin(part):
            return None if part is None else (swap(part, "dom", 1), swap(part, "dom", 2))

        mine = lax.dynamic_slice_in_dim(basis_image, me * (NZ // coil), NZ // coil, 2)
        mine = [mine] + [swap(mine, "dom", r) for r in (1, 2, 3)]
        first = begin(parts[0])
        mine, parts[1] = lax.optimization_barrier((mine, parts[1]))
        mine = jnp.stack(mine)
        second = begin(parts[1])
        there = swap(mine, "coil", 2)
        third = swap(first[1], "dom", 1)
        there, weights, third, first, second = lax.optimization_barrier(
            (there, weights, third, first, second)
        )
        both = jnp.stack([mine, there])
        images = [both, swap(both, "coil", 1)]
        total = None
        for m in range(len(sizes)):
            maps = [parts[m], *first, third]
            images, maps, second, parts[m + 2], total = lax.optimization_barrier(
                (images, maps, second, parts[m + 2], total)
            )
            if second is not None:
                third = swap(second[1], "dom", 1)
            first, second = second, begin(parts[m + 2])
            total = coils(maps, images, weights, tables, total, m == len(sizes) - 1, where)
    else:
        images = [lax.all_gather(basis_image, "dom", axis=3, tiled=True)[None, None]]
        maps = [lax.all_gather(coil_maps, "dom", axis=3, tiled=True)]
        total = coils(maps, images, weights, tables, None, True, where)

    def plus(a, b):
        return a.astype(F32) + b.astype(F32)

    keep, send = total
    total = plus(keep, swap(send, "coil", 1)).astype(BF)
    total = plus(total[0], swap(total[1], "coil", 2)).astype(BF)
    if not butterfly:
        total = lax.psum_scatter(total, "dom", scatter_dimension=3, tiled=True)
        return total.astype(F32).transpose(1, 2, 0, 3, 4) - adjoint_data
    total = total.reshape(NZ // coil, 2, K, 2, 2, rows, ny)
    total = plus(total[:, :, :, :, 0], swap(total[:, :, :, :, 1], "dom", 1)).astype(BF)
    total = plus(total[:, :, :, 0], swap(total[:, :, :, 1], "dom", 2))
    return total.transpose(1, 2, 0, 3, 4) - adjoint_data


CHUNKS = (2, 3, 3, 4)


def solution(mesh):
    placed = (
        P(None, None, "slab", "dom", None),
        P(None, "coil", "slab", "dom", None),
        P(None, None, "dom", None),
        P(),
        P(),
        P(None, None, ("slab", "coil"), "dom", None),
    )
    return jax.shard_map(
        body,
        mesh=mesh,
        in_specs=placed,
        out_specs=P(None, None, ("slab", "coil"), "dom", None),
        check_vma=False,
    )
```

```python
import functools
import itertools
import math

import jax
import jax.numpy as jnp
import numpy as np
from jax import lax
from jax.experimental import pallas as pl
from jax.experimental.pallas import tpu as pltpu
from jax.sharding import PartitionSpec as P

K = 5
NZ = 8
BF = jnp.bfloat16
F32 = jnp.float32
HALF = math.sqrt(0.5)


def table(count_in, count_out, length, sign):
    phase = (np.arange(count_in)[:, None] * np.arange(count_out)[None, :] % length).astype(
        np.float32
    ) * np.float32(2.0 * math.pi / length)
    scale = 1.0 / math.sqrt(length)
    cosine = np.cos(phase) * np.float32(scale)
    sine = np.sin(phase) * np.float32(sign * scale)
    return np.stack([np.stack([cosine, -sine]), np.stack([sine, cosine])]).astype(BF)


def add(a, b):
    return (a[0] + b[0], a[1] + b[1])


def sub(a, b):
    return (a[0] - b[0], a[1] - b[1])


def add_turned(a, b, sign):
    return (a[0] - b[1], a[1] + b[0]) if sign > 0 else (a[0] + b[1], a[1] - b[0])


def four(v, sign):
    a, b = add(v[0], v[2]), sub(v[0], v[2])
    c, d = add(v[1], v[3]), sub(v[1], v[3])
    return [add(a, c), add_turned(b, d, sign), sub(a, c), add_turned(b, d, -sign)]


def eight(re, im, sign):
    v = list(zip(re, im))
    e, o = four(v[0::2], sign), four(v[1::2], sign)
    h = jnp.asarray(HALF, re[0].dtype)
    once = add_turned(o[1], o[1], sign)
    once = (once[0] * h, once[1] * h)
    thrice = add_turned((-o[3][0], -o[3][1]), o[3], sign)
    thrice = (thrice[0] * h, thrice[1] * h)
    out = [None] * 8
    for q, t in ((0, o[0]), (1, once), (3, thrice)):
        out[q], out[q + 4] = add(e[q], t), sub(e[q], t)
    out[2], out[6] = add_turned(e[2], o[2], sign), add_turned(e[2], o[2], -sign)
    return [x[0] for x in out], [x[1] for x in out]


def tree(terms):
    while len(terms) > 1:
        terms = [
            terms[i] + terms[i + 1] if i + 1 < len(terms) else terms[i]
            for i in range(0, len(terms), 2)
        ]
    return terms[0]


def coils_kernel(width, pieces, images, first, last, where, *refs):
    maps, refs = refs[:pieces], refs[pieces:]
    shared, refs = refs[:images], refs[images:]
    *weights_hbm, ty, tx, tix, tiy = refs[:6]
    rest = list(refs[6:])
    acc_in = None if first else rest.pop(0)
    outs, rest = (rest[:2], rest[2:]) if last else (rest[:1], rest[1:])
    image, rows, spec, mid, product, weights, sems, image_sems = rest[:8]
    acc = rest[8] if last else outs[0]
    nx, ny = tix.shape[1] // 2, tiy.shape[1] // 2
    tiles = width // 16
    step = pl.program_id(0)
    me = where[1]

    def fetch(part, q):
        return pltpu.make_async_copy(
            weights_hbm[part].at[q], weights.at[part, q], sems.at[2 * q + part]
        )

    resume = None if first else pltpu.make_async_copy(acc_in, acc, sems.at[2 * NZ])
    groups = image.shape[0]
    arrive = []
    for b, ref in enumerate(shared):
        for x in range(ref.shape[0]):
            slot = ((x ^ (me // 2)) * 2 + (b ^ (me % 2))) if groups > 1 else 0
            arrive.append(
                pltpu.make_async_copy(ref.at[x], image.at[slot], image_sems.at[len(arrive)])
            )

    @pl.when(step == 0)
    def _():
        for copy in arrive:
            copy.start()
        for q in range(NZ):
            fetch(0, q).start()
            fetch(1, q).start()
        if first:
            acc[...] = jnp.zeros_like(acc)
        else:
            resume.start()
        for copy in arrive:
            copy.wait()

    def image_of(part, j, z):
        group, plane = z // (NZ // groups), z % (NZ // groups)
        return jnp.concatenate(
            [image[group, r, part, j, plane] for r in range(image.shape[1])], axis=0
        )

    def maps_of(part, z):
        return jnp.concatenate([m[part, 0, z] for m in maps], axis=0)

    def forward(j, _):
        for z in range(NZ):
            mr, mi = maps_of(0, z), maps_of(1, z)
            ir, ii = image_of(0, j, z), image_of(1, j, z)
            product[j, z * nx : (z + 1) * nx] = jnp.concatenate(
                [mr * ir - mi * ii, mr * ii + mi * ir], axis=1
            )
        turned = jnp.dot(product[j], ty[...], preferred_element_type=F32).astype(BF)
        for z in range(NZ):
            rows[j, z] = turned[z * nx : (z + 1) * nx].T
        for t in range(tiles):
            a, b = pl.ds(t * 16, 16), pl.ds(width + t * 16, 16)
            re, im = eight(
                [rows[j, z, a].astype(F32) for z in range(NZ)],
                [rows[j, z, b].astype(F32) for z in range(NZ)],
                -1,
            )
            for q in range(NZ):
                mid[j, pl.ds(q * width + t * 16, 16)] = jnp.concatenate(
                    [re[q], im[q]], axis=1
                ).astype(BF)
        spec[j] = jnp.dot(mid[j], tx[...], preferred_element_type=F32).astype(BF)
        return 0

    for j in range(K):
        forward(j, 0)

    half = tx.shape[1] // 2

    def apply(q, t):
        a = pl.ds(t * 16, 16)
        at = pl.ds(pl.multiple_of(q * width + t * 16, 16), 16)
        sr = [spec[j, at, :half] for j in range(K)]
        si = [spec[j, at, half:] for j in range(K)]
        for k in range(K):
            re, im = [], []
            for j in range(K):
                kr, ki = weights[0, q, k, j, a], weights[1, q, k, j, a]
                re.append(kr * sr[j] - ki * si[j])
                im.append(kr * si[j] + ki * sr[j])
            spec[k, at, :half] = tree(re)
            spec[k, at, half:] = tree(im)

    def apply_all(q, _):
        @pl.when(step == 0)
        def _():
            fetch(0, q).wait()
            fetch(1, q).wait()

        for t in range(tiles):
            apply(q, t)
        return 0

    lax.fori_loop(0, NZ, apply_all, 0)
    if not first:

        @pl.when(step == 0)
        def _():
            resume.wait()


    def inverse(k, _):
        mid[k] = jnp.dot(spec[k], tix[...], preferred_element_type=F32).astype(BF)
        for t in range(tiles):
            a, b = pl.ds(t * 16, 16), pl.ds(width + t * 16, 16)
            re, im = eight(
                [mid[k, pl.ds(q * width + t * 16, 16), :nx].astype(F32) for q in range(NZ)],
                [mid[k, pl.ds(q * width + t * 16, 16), nx:].astype(F32) for q in range(NZ)],
                1,
            )
            for z in range(NZ):
                rows[k, z, a] = re[z].astype(BF)
                rows[k, z, b] = im[z].astype(BF)
        turned = jnp.concatenate([rows[k, z].T for z in range(NZ)], axis=0)
        backs = jnp.dot(turned, tiy[...], preferred_element_type=F32)
        for z in range(NZ):
            back = backs[z * nx : (z + 1) * nx]
            br, bi = back[:, :ny], back[:, ny:]
            mr, mi = maps_of(0, z).astype(F32), maps_of(1, z).astype(F32)
            acc[z, 0, k] += mr * br + mi * bi
            acc[z, 1, k] += mr * bi - mi * br
        return 0

    for k in range(K):
        inverse(k, 0)
    if last:

        @pl.when(step == pl.num_programs(0) - 1)
        def _():
            low, high, block = outs[0].shape[2], outs[0].shape[3], outs[0].shape[6]
            for c, x, z, part in itertools.product(range(2), range(2), range(NZ // 4), range(2)):
                plane = (x ^ (me // 2)) * (NZ // 2) + (c ^ (me % 2)) * (NZ // 4) + z
                for lo, hi in itertools.product(range(low), range(high)):
                    a, b = (lo, x) if part == 1 and low == 2 else (x, lo)
                    at = (hi * low + lo) * block
                    outs[c][part, a, b, hi, :, z] = acc[plane, part, :, at : at + block].astype(BF)


def coils(maps, images, weights, tables, acc, last, where):
    count = maps[0].shape[1]
    spec_width = tables[1].shape[2]
    width = tables[0].shape[2] // 2
    nx, ny = tables[2].shape[2] // 2, tables[3].shape[2] // 2
    anywhere = pl.BlockSpec(memory_space=pl.ANY)
    shape = (NZ, 2, K, nx, ny)
    split = 2 if len(maps) == 4 else 1
    half = (2, 2, split, split, K, NZ // 4, nx // split**2, ny)
    out = [jax.ShapeDtypeStruct(half, BF)] * 2 if last else jax.ShapeDtypeStruct(shape, F32)
    block = lambda dims: pl.BlockSpec(
        dims, lambda c, w: (0,) * len(dims), pipeline_mode=pl.Buffered(buffer_count=1)
    )
    args = [*maps, *images, *weights, *tables]
    specs = [pl.BlockSpec((2, 1) + m.shape[2:], lambda c, w: (0, c, 0, 0, 0)) for m in maps]
    specs += [anywhere] * (len(images) + 2)
    specs += [
        pl.BlockSpec(
            (None,) + t.shape[1:],
            lambda c, w: (w[0], 0, 0),
            pipeline_mode=pl.Buffered(buffer_count=1),
        )
        for t in tables
    ]
    if acc is not None:
        args.append(acc)
        specs.append(anywhere)
    groups = sum(i.shape[0] for i in images)
    scratch = [
        pltpu.VMEM((groups,) + images[0].shape[1:], BF),
        pltpu.VMEM((K, NZ, 2 * width, nx), BF),
        pltpu.VMEM((K, NZ * width, spec_width), BF),
        pltpu.VMEM((K, NZ * width, 2 * nx), BF),
        pltpu.VMEM((K, NZ * nx, 2 * ny), BF),
        pltpu.VMEM((2,) + weights[0].shape, BF),
        pltpu.SemaphoreType.DMA((2 * NZ + 1,)),
        pltpu.SemaphoreType.DMA((groups,)),
    ]
    if last:
        scratch.append(pltpu.VMEM(shape, F32))
    planes = count * K * NZ
    return pl.pallas_call(
        functools.partial(coils_kernel, width, len(maps), len(images), acc is None, last),
        grid_spec=pltpu.PrefetchScalarGridSpec(
            num_scalar_prefetch=1,
            grid=(count,),
            in_specs=specs,
            out_specs=[block(half)] * 2 if last else block(shape),
            scratch_shapes=scratch,
        ),
        out_shape=out,
        compiler_params=pltpu.CompilerParams(vmem_limit_bytes=34 * 2**20),
        cost_estimate=pl.CostEstimate(
            flops=planes * width * 4 * 2 * 200_000, bytes_accessed=30_000_000, transcendentals=0
        ),
    )(where, *args)


def kernel_weights(sampled, basis_products, point_spread, pad):
    scale = float(table(1, 1, NZ, 1)[0, 0, 0, 0].astype(np.float32)) ** 2
    picked = basis_products[:, :, :, :, None] * (
        sampled.astype(F32)[:, None, None, None, :] * scale
    )
    real, imag = picked[:, 0], picked[:, 1]
    spread = point_spread.astype(BF)
    if pad:
        spread = jnp.pad(spread, ((0, 0), (0, 0), (0, pad), (0, 0)))
    return [
        jnp.einsum(
            "gikjq,givu->qkjvu",
            jnp.stack(pair, 1).astype(BF),
            spread,
            preferred_element_type=F32,
        ).astype(BF)
        for pair in ((real, -imag), (imag, real))
    ]


def swap(value, axis, bit):
    size = lax.axis_size(axis)
    return lax.ppermute(value, axis, [(i, i ^ bit) for i in range(size)])


def body(basis_image, coil_maps, point_spread, basis_products, sampled, adjoint_data):
    dom, here = lax.axis_size("dom"), lax.axis_index("dom")
    coil, me = lax.axis_size("coil"), lax.axis_index("coil")
    rows, ny = basis_image.shape[3], basis_image.shape[4]
    nx = rows * dom
    own = point_spread.shape[2]
    width = max(64, own)
    butterfly = dom == 4 and rows % 16 == 0

    forward, inverse = table(ny, 2 * ny, 2 * ny, -1), table(2 * ny, ny, 2 * ny, 1)
    extra = ((0, 0), (0, 0), (0, 0), (0, width - own))
    forward = np.pad(forward.transpose(1, 2, 0, 3), extra)
    inverse = np.pad(inverse.transpose(1, 0, 3, 2), extra).transpose(0, 3, 1, 2)
    ty = np.stack([forward[..., d * own : d * own + width] for d in range(dom)])
    tiy = np.stack([inverse[:, d * own : d * own + width] for d in range(dom)])
    forward, inverse = table(nx, 2 * nx, 2 * nx, -1), table(2 * nx, nx, 2 * nx, 1)
    tx = forward.transpose(1, 2, 0, 3).reshape(2, dom, rows, 4 * nx)
    tix = inverse.transpose(1, 2, 0, 3).reshape(4 * nx, 2, dom, rows)
    orders = [[d ^ r for r in range(dom)] if butterfly else range(dom) for d in range(dom)]
    if not butterfly:
        orders = orders[:1]
    tx = np.stack([tx[:, list(o)] for o in orders])
    tix = np.stack([tix[:, :, list(o)] for o in orders])
    if not butterfly:
        ty = lax.dynamic_slice_in_dim(jnp.asarray(ty), here, 1, 0)
        tiy = lax.dynamic_slice_in_dim(jnp.asarray(tiy), here, 1, 0)
    tables = [
        jnp.asarray(ty).reshape(-1, 2 * ny, 2 * width),
        jnp.asarray(tx).reshape(-1, 2 * nx, 4 * nx),
        jnp.asarray(tix).reshape(-1, 4 * nx, 2 * nx),
        jnp.asarray(tiy).reshape(-1, 2 * width, 2 * ny),
    ]
    where = jnp.stack([here if butterfly else 0 * here, me]).astype(jnp.int32)
    weights = kernel_weights(sampled, basis_products, point_spread, width - own)
    count = coil_maps.shape[1]

    if butterfly:
        sizes = CHUNKS if sum(CHUNKS) == count else (count,)
        starts = [sum(sizes[:m]) for m in range(len(sizes))]
        parts = [
            lax.slice_in_dim(coil_maps, a, a + n, axis=1) for a, n in zip(starts, sizes)
        ]
        fence = lax.optimization_barrier

        mine = lax.dynamic_slice_in_dim(basis_image, me * (NZ // coil), NZ // coil, 2)
        mine = [mine] + [swap(mine, "dom", r) for r in (1, 2, 3)]
        mine, weights[0], parts = fence((mine, weights[0], parts))
        mine = jnp.stack(mine)
        there = swap(mine, "coil", 2)
        one, two = swap(parts[0], "dom", 1), swap(parts[0], "dom", 2)
        ahead = [swap(p, "dom", 2) for p in parts[1:2]]
        there, weights[1], one, two, ahead, parts = fence(
            (there, weights[1], one, two, ahead, parts)
        )
        both = jnp.stack([mine, there])
        images = [both, swap(both, "coil", 1)]
        held = [one, two, swap(two, "dom", 1)]
        total = None
        for m in range(len(sizes)):
            images, held, ahead, parts, total = fence((images, held, ahead, parts, total))
            maps, held = [parts[m], *held], []
            if ahead:
                held = [swap(parts[m + 1], "dom", 1), ahead[0], swap(ahead[0], "dom", 1)]
                ahead = [swap(p, "dom", 2) for p in parts[m + 2 : m + 3]]
            total = coils(maps, images, weights, tables, total, m == len(sizes) - 1, where)
    else:
        images = [lax.all_gather(basis_image, "dom", axis=3, tiled=True)[None, None]]
        maps = [lax.all_gather(coil_maps, "dom", axis=3, tiled=True)]
        total = coils(maps, images, weights, tables, None, True, where)

    def plus(a, b):
        return a.astype(F32) + b.astype(F32)

    def half(value, axis, bit):
        return plus(value[0], swap(value[1], axis, bit)).astype(BF)

    keep, send = total
    total = plus(keep, swap(send, "coil", 1)).astype(BF)
    if not butterfly:
        total = plus(total[:, 0], swap(total[:, 1], "coil", 2)).astype(BF)
        total = lax.psum_scatter(total[:, 0, 0], "dom", scatter_dimension=3, tiled=True)
        return total.astype(F32) - adjoint_data
    real, imag = half(total[0], "coil", 2), half(total[1], "dom", 1)
    real, imag = half(real, "dom", 1), half(imag, "coil", 2)
    there = swap(jnp.stack([real[1], imag[1]]), "dom", 2)
    return jnp.stack([plus(real[0], there[0]), plus(imag[0], there[1])]) - adjoint_data


CHUNKS = (2, 3, 3, 4)


def solution(mesh):
    placed = (
        P(None, None, "slab", "dom", None),
        P(None, "coil", "slab", "dom", None),
        P(None, None, "dom", None),
        P(),
        P(),
        P(None, None, ("slab", "coil"), "dom", None),
    )
    return jax.shard_map(
        body,
        mesh=mesh,
        in_specs=placed,
        out_specs=P(None, None, ("slab", "coil"), "dom", None),
        check_vma=False,
    )
```

```python
import functools
import itertools
import math

import jax
import jax.numpy as jnp
import numpy as np
from jax import lax
from jax.experimental import pallas as pl
from jax.experimental.pallas import tpu as pltpu
from jax.sharding import PartitionSpec as P

K = 5
NZ = 8
BF = jnp.bfloat16
F32 = jnp.float32
HALF = math.sqrt(0.5)


def table(count_in, count_out, length, sign):
    phase = (np.arange(count_in)[:, None] * np.arange(count_out)[None, :] % length).astype(
        np.float32
    ) * np.float32(2.0 * math.pi / length)
    scale = 1.0 / math.sqrt(length)
    cosine = np.cos(phase) * np.float32(scale)
    sine = np.sin(phase) * np.float32(sign * scale)
    return np.stack([np.stack([cosine, -sine]), np.stack([sine, cosine])]).astype(BF)


def add(a, b):
    return (a[0] + b[0], a[1] + b[1])


def sub(a, b):
    return (a[0] - b[0], a[1] - b[1])


def add_turned(a, b, sign):
    return (a[0] - b[1], a[1] + b[0]) if sign > 0 else (a[0] + b[1], a[1] - b[0])


def four(v, sign):
    a, b = add(v[0], v[2]), sub(v[0], v[2])
    c, d = add(v[1], v[3]), sub(v[1], v[3])
    return [add(a, c), add_turned(b, d, sign), sub(a, c), add_turned(b, d, -sign)]


def eight(re, im, sign):
    v = list(zip(re, im))
    e, o = four(v[0::2], sign), four(v[1::2], sign)
    h = jnp.asarray(HALF, re[0].dtype)
    once = add_turned(o[1], o[1], sign)
    once = (once[0] * h, once[1] * h)
    thrice = add_turned((-o[3][0], -o[3][1]), o[3], sign)
    thrice = (thrice[0] * h, thrice[1] * h)
    out = [None] * 8
    for q, t in ((0, o[0]), (1, once), (3, thrice)):
        out[q], out[q + 4] = add(e[q], t), sub(e[q], t)
    out[2], out[6] = add_turned(e[2], o[2], sign), add_turned(e[2], o[2], -sign)
    return [x[0] for x in out], [x[1] for x in out]


def tree(terms):
    while len(terms) > 1:
        terms = [
            terms[i] + terms[i + 1] if i + 1 < len(terms) else terms[i]
            for i in range(0, len(terms), 2)
        ]
    return terms[0]


def coils_kernel(width, pieces, images, first, last, where, *refs):
    maps, refs = refs[:pieces], refs[pieces:]
    shared, refs = refs[:images], refs[images:]
    *weights_hbm, ty, tx, tix, tiy = refs[:6]
    rest = list(refs[6:])
    acc_in = None if first else rest.pop(0)
    outs, rest = (rest[:2], rest[2:]) if last else (rest[:1], rest[1:])
    image, rows, spec, mid, product, weights, sems, image_sems = rest[:8]
    acc = rest[8] if last else outs[0]
    nx, ny = tix.shape[1] // 2, tiy.shape[1] // 2
    tiles = width // 16
    step = pl.program_id(0)
    me = where[1]

    def fetch(part, q):
        return pltpu.make_async_copy(
            weights_hbm[part].at[q], weights.at[part, q], sems.at[2 * q + part]
        )

    resume = None if first else pltpu.make_async_copy(acc_in, acc, sems.at[2 * NZ])
    groups = image.shape[0]
    arrive = []
    for b, ref in enumerate(shared):
        for x in range(ref.shape[0]):
            slot = ((x ^ (me // 2)) * 2 + (b ^ (me % 2))) if groups > 1 else 0
            arrive.append(
                pltpu.make_async_copy(ref.at[x], image.at[slot], image_sems.at[len(arrive)])
            )

    @pl.when(step == 0)
    def _():
        for copy in arrive:
            copy.start()
        for q in range(NZ):
            fetch(0, q).start()
            fetch(1, q).start()
        if first:
            acc[...] = jnp.zeros_like(acc)
        else:
            resume.start()
        for copy in arrive:
            copy.wait()

    def image_of(part, j, z):
        group, plane = z // (NZ // groups), z % (NZ // groups)
        return jnp.concatenate(
            [image[group, r, part, j, plane] for r in range(image.shape[1])], axis=0
        )

    def maps_of(part, z):
        return jnp.concatenate([m[part, 0, z] for m in maps], axis=0)

    def forward(j, _):
        for z in range(NZ):
            mr, mi = maps_of(0, z), maps_of(1, z)
            ir, ii = image_of(0, j, z), image_of(1, j, z)
            product[j, z * nx : (z + 1) * nx] = jnp.concatenate(
                [mr * ir - mi * ii, mr * ii + mi * ir], axis=1
            )
        turned = jnp.dot(product[j], ty[...], preferred_element_type=F32).astype(BF)
        for z in range(NZ):
            rows[j, z] = turned[z * nx : (z + 1) * nx].T
        for t in range(tiles):
            a, b = pl.ds(t * 16, 16), pl.ds(width + t * 16, 16)
            re, im = eight(
                [rows[j, z, a].astype(F32) for z in range(NZ)],
                [rows[j, z, b].astype(F32) for z in range(NZ)],
                -1,
            )
            for q in range(NZ):
                mid[j, pl.ds(q * width + t * 16, 16)] = jnp.concatenate(
                    [re[q], im[q]], axis=1
                ).astype(BF)
        spec[j] = jnp.dot(mid[j], tx[...], preferred_element_type=F32).astype(BF)
        return 0

    for j in range(K):
        forward(j, 0)

    half = tx.shape[1] // 2

    def apply(q, t):
        a = pl.ds(t * 16, 16)
        at = pl.ds(pl.multiple_of(q * width + t * 16, 16), 16)
        sr = [spec[j, at, :half] for j in range(K)]
        si = [spec[j, at, half:] for j in range(K)]
        for k in range(K):
            re, im = [], []
            for j in range(K):
                kr, ki = weights[0, q, k, j, a], weights[1, q, k, j, a]
                re.append(kr * sr[j] - ki * si[j])
                im.append(kr * si[j] + ki * sr[j])
            spec[k, at, :half] = tree(re)
            spec[k, at, half:] = tree(im)

    def apply_all(q, _):
        @pl.when(step == 0)
        def _():
            fetch(0, q).wait()
            fetch(1, q).wait()

        for t in range(tiles):
            apply(q, t)
        return 0

    lax.fori_loop(0, NZ, apply_all, 0)
    if not first:

        @pl.when(step == 0)
        def _():
            resume.wait()


    def inverse(k, _):
        mid[k] = jnp.dot(spec[k], tix[...], preferred_element_type=F32).astype(BF)
        for t in range(tiles):
            a, b = pl.ds(t * 16, 16), pl.ds(width + t * 16, 16)
            re, im = eight(
                [mid[k, pl.ds(q * width + t * 16, 16), :nx].astype(F32) for q in range(NZ)],
                [mid[k, pl.ds(q * width + t * 16, 16), nx:].astype(F32) for q in range(NZ)],
                1,
            )
            for z in range(NZ):
                rows[k, z, a] = re[z].astype(BF)
                rows[k, z, b] = im[z].astype(BF)
        turned = jnp.concatenate([rows[k, z].T for z in range(NZ)], axis=0)
        backs = jnp.dot(turned, tiy[...], preferred_element_type=F32)
        for z in range(NZ):
            back = backs[z * nx : (z + 1) * nx]
            br, bi = back[:, :ny], back[:, ny:]
            mr, mi = maps_of(0, z).astype(F32), maps_of(1, z).astype(F32)
            acc[z, 0, k] += mr * br + mi * bi
            acc[z, 1, k] += mr * bi - mi * br
        return 0

    for k in range(K):
        inverse(k, 0)
    if last:

        @pl.when(step == pl.num_programs(0) - 1)
        def _():
            low, high, block = outs[0].shape[2], outs[0].shape[3], outs[0].shape[6]
            for c, x, z, part in itertools.product(range(2), range(2), range(NZ // 4), range(2)):
                plane = (x ^ (me // 2)) * (NZ // 2) + (c ^ (me % 2)) * (NZ // 4) + z
                for lo, hi in itertools.product(range(low), range(high)):
                    a, b = (lo, x) if part == 1 and low == 2 else (x, lo)
                    at = (hi * low + lo) * block
                    outs[c][part, a, b, hi, :, z] = acc[plane, part, :, at : at + block].astype(BF)


def coils(maps, images, weights, tables, acc, last, where):
    count = maps[0].shape[1]
    spec_width = tables[1].shape[2]
    width = tables[0].shape[2] // 2
    nx, ny = tables[2].shape[2] // 2, tables[3].shape[2] // 2
    anywhere = pl.BlockSpec(memory_space=pl.ANY)
    shape = (NZ, 2, K, nx, ny)
    split = 2 if len(maps) == 4 else 1
    half = (2, 2, split, split, K, NZ // 4, nx // split**2, ny)
    out = [jax.ShapeDtypeStruct(half, BF)] * 2 if last else jax.ShapeDtypeStruct(shape, F32)
    block = lambda dims: pl.BlockSpec(
        dims, lambda c, w: (0,) * len(dims), pipeline_mode=pl.Buffered(buffer_count=1)
    )
    args = [*maps, *images, *weights, *tables]
    specs = [pl.BlockSpec((2, 1) + m.shape[2:], lambda c, w: (0, c, 0, 0, 0)) for m in maps]
    specs += [anywhere] * (len(images) + 2)
    specs += [
        pl.BlockSpec(
            (None,) + t.shape[1:],
            lambda c, w: (w[0], 0, 0),
            pipeline_mode=pl.Buffered(buffer_count=1),
        )
        for t in tables
    ]
    if acc is not None:
        args.append(acc)
        specs.append(anywhere)
    groups = sum(i.shape[0] for i in images)
    scratch = [
        pltpu.VMEM((groups,) + images[0].shape[1:], BF),
        pltpu.VMEM((K, NZ, 2 * width, nx), BF),
        pltpu.VMEM((K, NZ * width, spec_width), BF),
        pltpu.VMEM((K, NZ * width, 2 * nx), BF),
        pltpu.VMEM((K, NZ * nx, 2 * ny), BF),
        pltpu.VMEM((2,) + weights[0].shape, BF),
        pltpu.SemaphoreType.DMA((2 * NZ + 1,)),
        pltpu.SemaphoreType.DMA((groups,)),
    ]
    if last:
        scratch.append(pltpu.VMEM(shape, F32))
    planes = count * K * NZ
    return pl.pallas_call(
        functools.partial(coils_kernel, width, len(maps), len(images), acc is None, last),
        grid_spec=pltpu.PrefetchScalarGridSpec(
            num_scalar_prefetch=1,
            grid=(count,),
            in_specs=specs,
            out_specs=[block(half)] * 2 if last else block(shape),
            scratch_shapes=scratch,
        ),
        out_shape=out,
        compiler_params=pltpu.CompilerParams(vmem_limit_bytes=34 * 2**20),
        cost_estimate=pl.CostEstimate(
            flops=planes * width * 4 * 2 * 200_000, bytes_accessed=30_000_000, transcendentals=0
        ),
    )(where, *args)


def kernel_weights(sampled, basis_products, point_spread, pad):
    scale = float(table(1, 1, NZ, 1)[0, 0, 0, 0].astype(np.float32)) ** 2
    picked = basis_products[:, :, :, :, None] * (
        sampled.astype(F32)[:, None, None, None, :] * scale
    )
    real, imag = picked[:, 0], picked[:, 1]
    spread = point_spread.astype(BF)
    if pad:
        spread = jnp.pad(spread, ((0, 0), (0, 0), (0, pad), (0, 0)))
    return [
        jnp.einsum(
            "gikjq,givu->qkjvu",
            jnp.stack(pair, 1).astype(BF),
            spread,
            preferred_element_type=F32,
        ).astype(BF)
        for pair in ((real, -imag), (imag, real))
    ]


def swap(value, axis, bit):
    size = lax.axis_size(axis)
    return lax.ppermute(value, axis, [(i, i ^ bit) for i in range(size)])


def body(basis_image, coil_maps, point_spread, basis_products, sampled, adjoint_data):
    dom, here = lax.axis_size("dom"), lax.axis_index("dom")
    coil, me = lax.axis_size("coil"), lax.axis_index("coil")
    rows, ny = basis_image.shape[3], basis_image.shape[4]
    nx = rows * dom
    own = point_spread.shape[2]
    width = max(64, own)
    butterfly = dom == 4 and rows % 16 == 0

    forward, inverse = table(ny, 2 * ny, 2 * ny, -1), table(2 * ny, ny, 2 * ny, 1)
    extra = ((0, 0), (0, 0), (0, 0), (0, width - own))
    forward = np.pad(forward.transpose(1, 2, 0, 3), extra)
    inverse = np.pad(inverse.transpose(1, 0, 3, 2), extra).transpose(0, 3, 1, 2)
    ty = np.stack([forward[..., d * own : d * own + width] for d in range(dom)])
    tiy = np.stack([inverse[:, d * own : d * own + width] for d in range(dom)])
    forward, inverse = table(nx, 2 * nx, 2 * nx, -1), table(2 * nx, nx, 2 * nx, 1)
    tx = forward.transpose(1, 2, 0, 3).reshape(2, dom, rows, 4 * nx)
    tix = inverse.transpose(1, 2, 0, 3).reshape(4 * nx, 2, dom, rows)
    orders = [[d ^ r for r in range(dom)] if butterfly else range(dom) for d in range(dom)]
    if not butterfly:
        orders = orders[:1]
    tx = np.stack([tx[:, list(o)] for o in orders])
    tix = np.stack([tix[:, :, list(o)] for o in orders])
    tables = [
        ty.reshape(-1, 2 * ny, 2 * width),
        tx.reshape(-1, 2 * nx, 4 * nx),
        tix.reshape(-1, 4 * nx, 2 * nx),
        tiy.reshape(-1, 2 * width, 2 * ny),
    ]
    tables = [
        jnp.asarray(t)
        if t.shape[0] == 1
        else lax.dynamic_index_in_dim(jnp.asarray(t), here, 0, keepdims=True)
        for t in tables
    ]
    where = jnp.stack([0 * here, me]).astype(jnp.int32)
    weights = kernel_weights(sampled, basis_products, point_spread, width - own)
    count = coil_maps.shape[1]

    if butterfly:
        sizes = CHUNKS if sum(CHUNKS) == count else (count,)
        starts = [sum(sizes[:m]) for m in range(len(sizes))]
        parts = [
            lax.slice_in_dim(coil_maps, a, a + n, axis=1) for a, n in zip(starts, sizes)
        ]
        fence = lax.optimization_barrier

        mine = lax.dynamic_slice_in_dim(basis_image, me * (NZ // coil), NZ // coil, 2)
        mine = [mine] + [swap(mine, "dom", r) for r in (1, 2, 3)]
        mine, weights[0], parts, tables = fence((mine, weights[0], parts, tables))
        mine = jnp.stack(mine)
        there = swap(mine, "coil", 2)
        one, two = swap(parts[0], "dom", 1), swap(parts[0], "dom", 2)
        ahead = [swap(p, "dom", 2) for p in parts[1:2]]
        there, weights[1], one, two, ahead, parts = fence(
            (there, weights[1], one, two, ahead, parts)
        )
        both = jnp.stack([mine, there])
        images = [both, swap(both, "coil", 1)]
        held = [one, two, swap(two, "dom", 1)]
        total = None
        for m in range(len(sizes)):
            images, held, ahead, parts, total = fence((images, held, ahead, parts, total))
            maps, held = [parts[m], *held], []
            if ahead:
                held = [swap(parts[m + 1], "dom", 1), ahead[0], swap(ahead[0], "dom", 1)]
                ahead = [swap(p, "dom", 2) for p in parts[m + 2 : m + 3]]
            total = coils(maps, images, weights, tables, total, m == len(sizes) - 1, where)
    else:
        images = [lax.all_gather(basis_image, "dom", axis=3, tiled=True)[None, None]]
        maps = [lax.all_gather(coil_maps, "dom", axis=3, tiled=True)]
        total = coils(maps, images, weights, tables, None, True, where)

    def plus(a, b):
        return a.astype(F32) + b.astype(F32)

    def half(value, axis, bit):
        return plus(value[0], swap(value[1], axis, bit)).astype(BF)

    keep, send = total
    total = plus(keep, swap(send, "coil", 1)).astype(BF)
    if not butterfly:
        total = plus(total[:, 0], swap(total[:, 1], "coil", 2)).astype(BF)
        total = lax.psum_scatter(total[:, 0, 0], "dom", scatter_dimension=3, tiled=True)
        return total.astype(F32) - adjoint_data
    real, imag = half(total[0], "coil", 2), half(total[1], "dom", 1)
    real, imag = half(real, "dom", 1), half(imag, "coil", 2)
    there = swap(jnp.stack([real[1], imag[1]]), "dom", 2)
    return jnp.stack([plus(real[0], there[0]), plus(imag[0], there[1])]) - adjoint_data


CHUNKS = (2, 3, 3, 4)


def solution(mesh):
    placed = (
        P(None, None, "slab", "dom", None),
        P(None, "coil", "slab", "dom", None),
        P(None, None, "dom", None),
        P(),
        P(),
        P(None, None, ("slab", "coil"), "dom", None),
    )
    return jax.shard_map(
        body,
        mesh=mesh,
        in_specs=placed,
        out_specs=P(None, None, ("slab", "coil"), "dom", None),
        check_vma=False,
    )
```
